32 devices in a mesh: parts: 2 (over x), blk: 4 (over y, core), rows: 4 (over z).
Axes of the slice: x: 2, y: 2, z: 4, core: 2. Of those that a mesh axis runs over, the one named last changes fastest.
Arguments:
- features: bfloat16 [8192, 512], P(('parts', 'blk', 'rows')), parts along dimension 0, may hold values from -6 to 6
- w_message: bfloat16 [512, 512], replicated, may hold values from -0.25 to 0.25
- w_update: bfloat16 [512, 512], replicated, may hold values from -0.25 to 0.25
- block_index: int32 [64, 40], P(('parts', 'blk', 'rows')), parts along dimension 0, may hold values from 0 to 31, as said below
- slot_count: int32 [64], P(('parts', 'blk', 'rows')), parts along dimension 0, may hold values from 10 to 40, as said below
- edge_count: int32 [64, 40, 128, 128], P(('parts', 'blk', 'rows')), parts along dimension 0, may hold values from 0 to 2
- cotangent: bfloat16 [8192, 512], P(('parts', 'blk', 'rows')), parts along dimension 0, may hold values from -6 to 6
Outputs:
- updated: bfloat16 [8192, 512], P(('parts', 'blk', 'rows')), parts along dimension 0
- d_features: bfloat16 [8192, 512], P(('parts', 'blk', 'rows')), parts along dimension 0
- grad_message: float32 [1024, 512], P('parts'), parts along dimension 0
- grad_update: float32 [1024, 512], P('parts'), parts along dimension 0
The draws below stay inside these ranges and needn't reach their ends.
There are 2 independent parts, one for each index of `parts`. The reference program is written for one: setup_inputs(seed, part) draws one part's arguments, and reference() takes and returns one part's arrays. A program takes and returns all parts, laid end to end along the dimension named above; an argument that names none is the same for every part. Nothing has to cross between parts.
Inputs may be any that keep to these rules, and one draw needn't show every extreme that they name: `block_index`: the source blocks of a block row lie in its own region or in the two regions beside it on the periodic chain; block b lies in region b // 8. `slot_count`: some block row uses all 40 slots in every draw.
All inputs are finite; a program needn't handle non-finite values.
Results may differ from the reference program's by a relative error of at most 0.015.
Values may be sent and summed in bfloat16 or wider, within the bound.
A program may use at most 128 MiB of HBM per device.

```python
import math
import jax
import jax.numpy as jnp
from jax import lax

D = 512
TILE = 128
BLK_DEV = 2
MAXB = 40
REGIONS = 4
REGION_BLOCKS = 8
BLOCKS = 32
NODES = 4096
N_ROWS = 4


def draw_block_index(key, part):
    key = jax.random.fold_in(key, 11)
    key_side, key_offset = jax.random.split(key)
    side = jax.random.randint(key_side, (BLOCKS, MAXB), 0, 3)
    offset = jax.random.randint(key_offset, (BLOCKS, MAXB), 0, REGION_BLOCKS)
    region = jnp.arange(BLOCKS, dtype=jnp.int32) // REGION_BLOCKS
    source = jnp.mod(region[:, None] + side - 1, REGIONS) * REGION_BLOCKS + offset
    return source.astype(jnp.int32)


def draw_slot_count(key, part):
    key = jax.random.fold_in(key, 23)
    key_heavy, key_high, key_low = jax.random.split(key, 3)
    heavy = jax.random.randint(key_heavy, (REGIONS,), 0, 2)
    high_load = jax.random.randint(key_high, (BLOCKS,), MAXB // 2, MAXB + 1)
    low_load = jax.random.randint(key_low, (BLOCKS,), MAXB // 4, MAXB // 2 + 1)
    region = jnp.arange(BLOCKS, dtype=jnp.int32) // REGION_BLOCKS
    counts = jnp.where(heavy[region] == 1, high_load, low_load)
    counts = counts.at[0].set(MAXB)
    return counts.astype(jnp.int32)


def draw_edge_count(key, part):
    key = jax.random.fold_in(key, 37)
    key_face, key_mult = jax.random.split(key)
    span = MAXB * TILE
    hits = min(span // 2, 32)
    shape = (BLOCKS, MAXB, TILE, TILE)
    present = jax.random.randint(key_face, shape, 0, span) < hits
    multiple = jax.random.randint(key_mult, shape, 1, 3)
    return jnp.where(present, multiple, 0).astype(jnp.int32)


def level_of(rng, dims, cuts, low, largest):
    def one(position, blocks):
        steps = jax.random.uniform(jax.random.fold_in(jax.random.fold_in(rng, 6), position), (blocks,), jnp.float32, low / len(cuts), largest / len(cuts))
        return jnp.repeat(jnp.exp(steps), dims[position] // blocks).reshape((-1,) + (1,) * (len(dims) - position - 1))

    loudness = one(*cuts[0])
    for cut in cuts[1:]:
        loudness = loudness * one(*cut)
    return loudness


def bell_draw(key, shape, width, limit, cuts=(), kind=jnp.bfloat16):
    drawn = jax.random.normal(key, shape, jnp.float32) * width
    if len(cuts) > 0:
        drawn = level_of(key, shape, cuts, -0.22, 0.18) * drawn
    return jnp.clip(drawn, min=-limit, max=limit).astype(kind)


def setup_inputs(seed: int = 0, part: int = 0) -> dict:
    key_list = jax.random.split(jax.random.key(seed), 8)
    part_keys = jax.random.split(jax.random.fold_in(key_list[7], part), 8)
    features = bell_draw(part_keys[0], (NODES, D), 1.0, 6.0, ((0, 16),))
    w_message = bell_draw(key_list[1], (D, D), D ** -0.5, 0.25)
    w_update = bell_draw(key_list[2], (D, D), D ** -0.5, 0.25)
    block_index = draw_block_index(jax.random.fold_in(jax.random.fold_in(key_list[7], part), 71), part)
    slot_count = draw_slot_count(jax.random.fold_in(jax.random.fold_in(key_list[7], part), 71), part)
    edge_count = draw_edge_count(jax.random.fold_in(jax.random.fold_in(key_list[7], part), 71), part)
    cotangent = bell_draw(part_keys[6], (NODES, D), 1.0, 6.0, ((0, 16),))
    return {"features": features, "w_message": w_message, "w_update": w_update, "block_index": block_index, "slot_count": slot_count, "edge_count": edge_count, "cotangent": cotangent}


def reference(features, w_message, w_update, block_index, slot_count, edge_count, cotangent):
    hidden = jnp.dot(features, w_message, preferred_element_type=jnp.float32).astype(jnp.bfloat16)
    hidden_blocks = hidden.reshape(BLOCKS, TILE, D)
    slot_valid = jnp.arange(MAXB, dtype=jnp.int32)[None, :] < slot_count[:, None]
    counts = jnp.where(slot_valid[:, :, None, None], edge_count, jnp.int32(0))
    counts_f = counts.astype(jnp.float32)
    row_norm = jnp.sqrt(1.0 + lax.optimization_barrier(jnp.sum(counts_f * counts_f, axis=(1, 3))))

    def aggregate(pieces):
        block_ids, tile_counts = pieces
        sources = hidden_blocks[block_ids].astype(jnp.float32)
        return jnp.einsum('bsij,bsjd->bid', tile_counts.astype(jnp.float32), sources)
    summed = lax.map(aggregate, (block_index.reshape(REGIONS, REGION_BLOCKS, MAXB), counts.reshape(REGIONS, REGION_BLOCKS, MAXB, TILE, TILE)))
    message = summed.reshape(BLOCKS, TILE, D) / row_norm[:, :, None]
    smooth = jax.nn.silu(message).astype(jnp.bfloat16).reshape(NODES, D)
    updated = (features.astype(jnp.float32) + jnp.dot(smooth, w_update, preferred_element_type=jnp.float32)).astype(jnp.bfloat16)
    grad_scale = 1.0 / math.sqrt(NODES)
    grad_update = jnp.dot(smooth.T, cotangent, preferred_element_type=jnp.float32) * grad_scale
    d_smooth = jnp.dot(cotangent, w_update.T, preferred_element_type=jnp.float32).reshape(BLOCKS, TILE, D)
    sigmoid_m = jax.nn.sigmoid(message)
    d_message = (d_smooth * sigmoid_m * (1.0 + message * (1.0 - sigmoid_m)) / row_norm[:, :, None]).astype(jnp.bfloat16)
    devices = REGIONS * N_ROWS

    def add_device(running, pieces):
        block_ids, tile_counts, d_msg = pieces
        contrib = jnp.einsum('bsij,bid->bsjd', tile_counts.astype(jnp.float32), d_msg.astype(jnp.float32))
        partial_value = jnp.zeros((BLOCKS, TILE, D), jnp.float32).at[block_ids.reshape(-1)].add(contrib.reshape(-1, TILE, D))
        rounded = lax.optimization_barrier(partial_value.astype(jnp.bfloat16))
        return (running + rounded.astype(jnp.float32), None)
    running, unused = lax.scan(add_device, jnp.zeros((BLOCKS, TILE, D), jnp.float32), (block_index.reshape(devices, BLK_DEV, MAXB), counts.reshape(devices, BLK_DEV, MAXB, TILE, TILE), d_message.reshape(devices, BLK_DEV, TILE, D)))
    d_hidden = running.reshape(NODES, D).astype(jnp.bfloat16)
    d_features = (cotangent.astype(jnp.float32) + jnp.dot(d_hidden, w_message.T, preferred_element_type=jnp.float32)).astype(jnp.bfloat16)
    grad_message = jnp.dot(features.T, d_hidden, preferred_element_type=jnp.float32) * grad_scale
    return (updated, d_features, grad_message, grad_update)
```

```python
import functools
import math

import jax
import jax.numpy as jnp
from jax import lax
from jax.experimental import pallas as pl
from jax.experimental.pallas import tpu as pltpu
from jax.sharding import PartitionSpec as P

MESH = pl.DeviceIdType.MESH
F32 = jnp.float32
BF16 = jnp.bfloat16
SLOT_STEP = 8


def partner(z, j):
    out, bit = z, 1
    while bit <= j:
        if j & bit:
            out = out + bit * (1 - 2 * ((z // bit) % 2))
        bit *= 2
    return out


def dense_kernel(nb, region_blocks, index_ref, count_ref, edge_ref, a_ref, sq_ref):
    b = pl.program_id(0)
    step = pl.program_id(1)
    r = lax.axis_index("blk")
    tile = edge_ref.shape[2]

    @pl.when((b == 0) & (step == 0))
    def _():
        a_ref[...] = jnp.zeros_like(a_ref)
        sq_ref[...] = jnp.zeros_like(sq_ref)

    rows = pl.ds(pl.multiple_of(b * tile, tile), tile)
    used = count_ref[b]
    for i in range(edge_ref.shape[1]):
        s = step * edge_ref.shape[1] + i

        @pl.when(s < used)
        def _():
            total = nb * region_blocks
            k = lax.rem(index_ref[b, s] - (r - 1) * region_blocks + 2 * total, total)
            c = edge_ref[0, i].astype(BF16)
            a_ref[k, rows, :] += c
            sq_ref[rows, :] += c * c


def dense(block_index, slot_count, edge_count, nb, nr):
    lb, slots = block_index.shape
    tile = edge_count.shape[2]
    step = SLOT_STEP if slots % SLOT_STEP == 0 else 1
    region_blocks = lb * nr
    return pl.pallas_call(
        functools.partial(dense_kernel, nb, region_blocks),
        grid=(lb, slots // step),
        out_shape=(
            jax.ShapeDtypeStruct((3 * region_blocks, lb * tile, tile), BF16),
            jax.ShapeDtypeStruct((lb * tile, tile), BF16),
        ),
        in_specs=[
            pl.BlockSpec(memory_space=pltpu.SMEM),
            pl.BlockSpec(memory_space=pltpu.SMEM),
            pl.BlockSpec((1, step, tile, tile), lambda b, s: (b, s, 0, 0)),
        ],
        out_specs=(
            pl.BlockSpec((3 * region_blocks, lb * tile, tile), lambda b, s: (0, 0, 0)),
            pl.BlockSpec((lb * tile, tile), lambda b, s: (0, 0)),
        ),
        compiler_params=pltpu.CompilerParams(vmem_limit_bytes=32 * 1024 * 1024),
    )(block_index, slot_count, edge_count)


def layer_kernel(
    nb, nr, lb,
    a_ref, sq_ref, x_ref, cot_ref, wm_ref, wu_ref,
    upd_ref, df_ref, gout,
    xwin, qs, qr, ss, sr, acc, ds, g, grecv, hbuf, yrecv, h2, zrecv,
    s1, r1, sf, rf, sq_s, sq_r, st_s, st_r,
    sp, rp, sy, ry, sz, rz, sa, ra, sb, rb, sm, rm,
):
    z = lax.axis_index("rows")
    r = lax.axis_index("blk")
    ny = nb // 2
    c = lax.rem(r, 2)
    yy = r // 2
    mate = yy * 2 + (1 - c)
    up, down = lax.rem(r + 1, nb), lax.rem(r + nb - 1, nb)
    row_peer = [partner(z, j) for j in range(nr)]
    y_peer = [lax.rem(yy + i, ny) for i in range(ny)]
    y_from = [lax.rem(yy + ny - i, ny) for i in range(ny)]

    def copy(src, dst, send, recv, where):
        return pltpu.make_async_remote_copy(
            src_ref=src, dst_ref=dst, send_sem=send, recv_sem=recv,
            device_id=where, device_id_type=MESH,
        )

    barrier = pltpu.get_barrier_semaphore()
    peers = [{"rows": row_peer[j]} for j in range(1, nr)]
    peers += [{"blk": up}, {"blk": down}]
    peers += [{"blk": lax.rem(r + 2 * i, nb)} for i in range(1, ny)]
    for where in peers:
        pl.semaphore_signal(barrier, inc=1, device_id=where, device_id_type=MESH)
    pl.semaphore_wait(barrier, len(peers))

    sends = []

    def start(*args):
        one = copy(*args)
        one.start()
        sends.append(one)

    def forward(j):
        src = x_ref if j == 0 else xwin.at[nr + row_peer[j]]
        start(src, xwin.at[row_peer[j]], sf.at[0, j], rf.at[0, j], {"blk": up})
        start(src, xwin.at[2 * nr + row_peer[j]], sf.at[1, j], rf.at[1, j], {"blk": down})

    forward(0)
    for j in range(1, nr):
        start(x_ref, xwin.at[nr + z], s1.at[j - 1], r1.at[j - 1], {"rows": row_peer[j]})

    def tiles(side, shard):
        first = (side * nr + shard) * lb
        return jnp.concatenate([a_ref[first + i] for i in range(lb)], axis=1)

    def mm(a, b):
        return jnp.dot(a, b, preferred_element_type=F32)

    def mm_t(a, b):
        return lax.dot_general(a, b, (((0,), (0,)), ((), ())), preferred_element_type=F32)

    def mm_bt(a, b):
        return lax.dot_general(a, b, (((1,), (1,)), ((), ())), preferred_element_type=F32)

    ds[...] = mm_bt(cot_ref[...], wu_ref[...])
    acc[...] = mm(tiles(1, z), x_ref[...])
    for j in range(1, nr):
        slot = nr + row_peer[j]
        copy(x_ref, xwin.at[slot], s1.at[j - 1], r1.at[j - 1], {"rows": row_peer[j]}).wait_recv()
        forward(j)
        acc[...] += mm(tiles(1, row_peer[j]), xwin[slot])
    for j in range(nr):
        for d, side, where in ((0, 0, up), (1, 2, down)):
            slot = side * nr + row_peer[j]
            copy(x_ref, xwin.at[slot], sf.at[d, j], rf.at[d, j], {"blk": where}).wait_recv()
            acc[...] += mm(tiles(side, row_peer[j]), xwin[slot])

    inv = 1.0 / jnp.sqrt(1.0 + jnp.sum(sq_ref[...].astype(F32), axis=1, keepdims=True))
    y = acc[...].astype(BF16)
    message = mm(y, wm_ref[...]) * inv
    sig = 1.0 / (1.0 + jnp.exp(-message))
    smooth = (message * sig).astype(BF16)
    d_message = (ds[...] * sig * (1.0 + message * (1.0 - sig)) * inv).astype(BF16)
    dz = mm_bt(d_message, wm_ref[...]).astype(BF16)
    ds[...] = dz.astype(F32)

    order = list(range(1, nr)) + [0]
    for j in order:
        for d, side, where in ((0, 2, up), (1, 0, down)):
            qs[d, j] = mm_t(tiles(side, row_peer[j]), dz).astype(BF16)
            start(qs.at[d, j], qr.at[d, j], sq_s.at[d, j], sq_r.at[d, j], {"blk": where})

    g[0] = mm_t(y, d_message).reshape(g.shape[1:]).astype(BF16)
    g[1] = mm_t(smooth, cot_ref[...]).reshape(g.shape[1:]).astype(BF16)
    start(g.at[1 - c], grecv, sp, rp, {"blk": mate})
    upd_ref[...] = (x_ref[...].astype(F32) + mm(smooth, wu_ref[...])).astype(BF16)
    copy(grecv, grecv, sp, rp, {"blk": mate}).wait_recv()
    hbuf[...] = (g[c].astype(F32) + grecv[...].astype(F32)).astype(BF16)
    for i in range(1, ny):
        start(hbuf.at[y_peer[i]], yrecv.at[i - 1], sy.at[i - 1], ry.at[i - 1], {"blk": 2 * y_peer[i] + c})

    def summed(j):
        total = mm_t(tiles(1, row_peer[j]), ds[...].astype(BF16))
        for d, where in ((0, up), (1, down)):
            copy(qs.at[d, j], qr.at[d, j], sq_s.at[d, j], sq_r.at[d, j], {"blk": where}).wait_recv()
            total += qr[d, j].astype(F32)
        return total

    for j in range(1, nr):
        ss[j - 1] = summed(j).astype(BF16)
        start(ss.at[j - 1], sr.at[j - 1], st_s.at[j - 1], st_r.at[j - 1], {"rows": row_peer[j]})

    part = hbuf[yy].astype(F32)
    for i in range(1, ny):
        copy(yrecv.at[i - 1], yrecv.at[i - 1], sy.at[i - 1], ry.at[i - 1], {"blk": 2 * y_peer[i] + c}).wait_recv()
        part += yrecv[i - 1].astype(F32)
    h2[...] = part.astype(BF16)
    for j in range(1, nr):
        start(h2.at[row_peer[j]], zrecv.at[j - 1], sz.at[j - 1], rz.at[j - 1], {"rows": row_peer[j]})

    acc[...] = summed(0) + cot_ref[...].astype(F32)

    piece = h2[z].astype(F32)
    for j in range(1, nr):
        copy(zrecv.at[j - 1], zrecv.at[j - 1], sz.at[j - 1], rz.at[j - 1], {"rows": row_peer[j]}).wait_recv()
        piece += zrecv[j - 1].astype(F32)
    gout[c, yy, z] = piece.astype(BF16)
    for j in range(1, nr):
        start(gout.at[c, yy, z], gout.at[c, yy, z], sa.at[j - 1], ra.at[j - 1], {"rows": row_peer[j]})

    for j in range(1, nr):
        copy(ss.at[j - 1], sr.at[j - 1], st_s.at[j - 1], st_r.at[j - 1], {"rows": row_peer[j]}).wait_recv()
        acc[...] += sr[j - 1].astype(F32)
    df_ref[...] = acc[...].astype(BF16)

    for j in range(1, nr):
        place = gout.at[c, yy, row_peer[j]]
        copy(place, place, sa.at[j - 1], ra.at[j - 1], {"rows": row_peer[j]}).wait_recv()
    for i in range(1, ny):
        start(gout.at[c, yy], gout.at[c, yy], sb.at[i - 1], rb.at[i - 1], {"blk": 2 * y_peer[i] + c})
    start(gout.at[c, yy], gout.at[c, yy], sm.at[0], rm.at[0], {"blk": mate})
    for i in range(1, ny):
        place = gout.at[c, y_from[i]]
        copy(place, place, sb.at[i - 1], rb.at[i - 1], {"blk": 2 * y_peer[i] + c}).wait_recv()
        start(place, place, sm.at[i], rm.at[i], {"blk": mate})
    for i in range(ny):
        place = gout.at[1 - c, y_from[i]]
        copy(place, place, sm.at[i], rm.at[i], {"blk": mate}).wait_recv()
    for one in sends:
        one.wait_send()


def body(features, w_message, w_update, block_index, slot_count, edge_count, cotangent):
    nr = lax.axis_size("rows")
    nb = lax.axis_size("blk")
    ny = nb // 2
    lb = block_index.shape[0]
    rows, width = features.shape
    a, sq = dense(block_index, slot_count, edge_count, nb, nr)
    pr = width // (ny * nr)
    shard = (rows, width)
    dma = pltpu.SemaphoreType.DMA
    vmem = pl.BlockSpec(memory_space=pltpu.VMEM)
    n1 = nr - 1
    updated, d_features, grads = pl.pallas_call(
        functools.partial(layer_kernel, nb, nr, lb),
        out_shape=(
            jax.ShapeDtypeStruct(shard, BF16),
            jax.ShapeDtypeStruct(shard, BF16),
            jax.ShapeDtypeStruct((2, ny, nr, pr, width), BF16),
        ),
        in_specs=[vmem] * 6,
        out_specs=(vmem,) * 3,
        scratch_shapes=[
            pltpu.VMEM((3 * nr,) + shard, BF16),
            pltpu.VMEM((2, nr) + shard, BF16),
            pltpu.VMEM((2, nr) + shard, BF16),
            pltpu.VMEM((n1,) + shard, BF16),
            pltpu.VMEM((n1,) + shard, BF16),
            pltpu.VMEM(shard, F32),
            pltpu.VMEM(shard, F32),
            pltpu.VMEM((2, ny, nr, pr, width), BF16),
            pltpu.VMEM((ny, nr, pr, width), BF16),
            pltpu.VMEM((ny, nr, pr, width), BF16),
            pltpu.VMEM((ny - 1, nr, pr, width), BF16),
            pltpu.VMEM((nr, pr, width), BF16),
            pltpu.VMEM((n1, pr, width), BF16),
            dma((n1,)), dma((n1,)),
            dma((2, nr)), dma((2, nr)),
            dma((2, nr)), dma((2, nr)),
            dma((n1,)), dma((n1,)),
            dma, dma,
            dma((ny - 1,)), dma((ny - 1,)),
            dma((n1,)), dma((n1,)),
            dma((n1,)), dma((n1,)),
            dma((ny - 1,)), dma((ny - 1,)),
            dma((ny,)), dma((ny,)),
        ],
        compiler_params=pltpu.CompilerParams(
            collective_id=0, has_side_effects=True, vmem_limit_bytes=48 * 1024 * 1024
        ),
    )(a, sq, features, cotangent, w_message, w_update)
    scale = 1.0 / math.sqrt(rows * nb * nr)
    grad_message = grads[0].reshape(width, width).astype(F32) * scale
    grad_update = grads[1].reshape(width, width).astype(F32) * scale
    return (updated, d_features, grad_message, grad_update)


def solution(mesh):
    placed = (
        P(("parts", "blk", "rows"), None),
        P(),
        P(),
        P(("parts", "blk", "rows"), None),
        P(("parts", "blk", "rows")),
        P(("parts", "blk", "rows"), None, None, None),
        P(("parts", "blk", "rows"), None),
    )
    return jax.shard_map(
        body,
        mesh=mesh,
        in_specs=placed,
        out_specs=(
            P(("parts", "blk", "rows"), None),
            P(("parts", "blk", "rows"), None),
            P("parts", None),
            P("parts", None),
        ),
        check_vma=False,
    )
```

```python
import functools
import math

import jax
import jax.numpy as jnp
from jax import lax
from jax.experimental import pallas as pl
from jax.experimental.pallas import tpu as pltpu
from jax.sharding import PartitionSpec as P

MESH = pl.DeviceIdType.MESH
F32 = jnp.float32
BF16 = jnp.bfloat16
SLOT_STEP = 8


def dense_kernel(nb, region_blocks, index_ref, count_ref, edge_ref, a_ref, sq_ref):
    b = pl.program_id(0)
    step = pl.program_id(1)
    r = lax.axis_index("blk")
    tile = edge_ref.shape[2]

    @pl.when((b == 0) & (step == 0))
    def _():
        a_ref[...] = jnp.zeros_like(a_ref)
        sq_ref[...] = jnp.zeros_like(sq_ref)

    rows = pl.ds(pl.multiple_of(b * tile, tile), tile)
    used = count_ref[b]
    for i in range(edge_ref.shape[1]):
        s = step * edge_ref.shape[1] + i

        @pl.when(s < used)
        def _():
            total = nb * region_blocks
            k = lax.rem(index_ref[b, s] - (r - 1) * region_blocks + 2 * total, total)
            c = edge_ref[0, i].astype(BF16)
            a_ref[k, rows, :] += c
            sq_ref[rows, :] += c * c


def dense(block_index, slot_count, edge_count, nb, nr):
    lb, slots = block_index.shape
    tile = edge_count.shape[2]
    step = SLOT_STEP if slots % SLOT_STEP == 0 else 1
    region_blocks = lb * nr
    return pl.pallas_call(
        functools.partial(dense_kernel, nb, region_blocks),
        grid=(lb, slots // step),
        out_shape=(
            jax.ShapeDtypeStruct((3 * region_blocks, lb * tile, tile), BF16),
            jax.ShapeDtypeStruct((lb * tile, tile), BF16),
        ),
        in_specs=[
            pl.BlockSpec(memory_space=pltpu.SMEM),
            pl.BlockSpec(memory_space=pltpu.SMEM),
            pl.BlockSpec((1, step, tile, tile), lambda b, s: (b, s, 0, 0)),
        ],
        out_specs=(
            pl.BlockSpec((3 * region_blocks, lb * tile, tile), lambda b, s: (0, 0, 0)),
            pl.BlockSpec((lb * tile, tile), lambda b, s: (0, 0)),
        ),
        compiler_params=pltpu.CompilerParams(vmem_limit_bytes=32 * 1024 * 1024),
    )(block_index, slot_count, edge_count)


def layer_kernel(
    nb, nr, lb,
    a_ref, sq_ref, x_ref, cot_ref, wm_ref, wu_ref,
    upd_ref, df_ref, gout,
    xwin, qs, qr, ss, sr, acc, ds, tot, dzb, smb, g, grecv, hbuf, yrecv, h2, zrecv,
    s1, r1, sf, rf, sq_s, sq_r, st_s, st_r,
    sp, rp, sy, ry, sz, rz, sa, ra, sb, rb, sm, rm,
):
    z = lax.axis_index("rows")
    r = lax.axis_index("blk")
    ny = nb // 2
    c = lax.rem(r, 2)
    yy = r // 2
    mate = yy * 2 + (1 - c)
    up, down = lax.rem(r + 1, nb), lax.rem(r + nb - 1, nb)
    others = [lax.rem(z + j, nr) for j in range(nr)]
    sources = [lax.rem(z + nr - j, nr) for j in range(nr)]
    y_peer = [lax.rem(yy + i, ny) for i in range(ny)]
    y_from = [lax.rem(yy + ny - i, ny) for i in range(ny)]

    def copy(src, dst, send, recv, where):
        return pltpu.make_async_remote_copy(
            src_ref=src, dst_ref=dst, send_sem=send, recv_sem=recv,
            device_id=where, device_id_type=MESH,
        )

    barrier = pltpu.get_barrier_semaphore()
    peers = [{"rows": others[j]} for j in range(1, nr)]
    peers += [{"blk": up}, {"blk": down}]
    peers += [{"blk": lax.rem(r + 2 * i, nb)} for i in range(1, ny)]
    for where in peers:
        pl.semaphore_signal(barrier, inc=1, device_id=where, device_id_type=MESH)
    pl.semaphore_wait(barrier, len(peers))

    sends = []

    def start(*args):
        start_when(None, lambda: args)

    def start_when(when, make):
        copy(*make()).start()
        sends.append((when, make))

    def guarded(when, run):
        if when is None:
            run()
        else:
            pl.when(when)(run)

    def forward(src, shard, when=None):
        for d, where in ((0, up), (1, down)):
            start_when(
                when,
                lambda d=d, where=where: (
                    src(), xwin.at[2 * d * nr + shard], sf.at[d, shard], rf.at[d, shard], {"blk": where}
                ),
            )

    def along(way, t):
        sign = 1 - 2 * way
        there = z + sign
        far = z + sign * t
        near = z - sign
        behind = z - sign * t
        has_there = (there >= 0) & (there < nr)
        has_far = (far >= 0) & (far < nr)
        has_near = (near >= 0) & (near < nr)
        has_behind = (behind >= 0) & (behind < nr)
        return there, has_there, far, has_far, has_near, behind, has_behind

    forward(lambda: x_ref, z)
    for way in range(2):
        there, has_there = along(way, 1)[:2]

        def first(way=way, there=there, has_there=has_there):
            start_when(
                has_there,
                lambda: (x_ref, xwin.at[nr + z], s1.at[way, 0], r1.at[way, 0], {"rows": there}),
            )

        pl.when(has_there)(first)

    def tiles(side, shard):
        first = (side * nr + shard) * lb
        return jnp.concatenate([a_ref[first + i] for i in range(lb)], axis=1)

    def mm(a, b):
        return jnp.dot(a, b, preferred_element_type=F32)

    def mm_t(a, b):
        return lax.dot_general(a, b, (((0,), (0,)), ((), ())), preferred_element_type=F32)

    def mm_bt(a, b):
        return lax.dot_general(a, b, (((1,), (1,)), ((), ())), preferred_element_type=F32)

    ds[...] = mm_bt(cot_ref[...], wu_ref[...])
    acc[...] = mm(tiles(1, z), x_ref[...])
    for t in range(1, nr):
        for way in range(2):
            there, has_there, far, has_far, has_near, behind, has_behind = along(way, t)

            def arrive(way=way, t=t, behind=behind):
                place = xwin.at[nr + behind]
                copy(place, place, s1.at[way, t - 1], r1.at[way, t - 1], {"blk": up}).wait_recv()

            def relay(way=way, t=t, there=there, behind=behind, when=has_there & has_behind):
                start_when(
                    when,
                    lambda: (
                        xwin.at[nr + behind], xwin.at[nr + behind], s1.at[way, t], r1.at[way, t], {"rows": there}
                    ),
                )

            def use(way=way, t=t, behind=behind, has_there=has_there, has_behind=has_behind, relay=relay, arrive=arrive):
                arrive()
                if t < nr - 1:
                    pl.when(has_there)(relay)
                forward(lambda: xwin.at[nr + behind], behind, has_behind)
                acc[...] += mm(tiles(1, behind), xwin[nr + behind])

            pl.when(has_behind)(use)

    def neighbour(shard):
        for d, side in ((0, 0), (1, 2)):
            slot = side * nr + shard
            copy(xwin.at[slot], xwin.at[slot], sf.at[d, shard], rf.at[d, shard], {"blk": up}).wait_recv()
            acc[...] += mm(tiles(side, shard), xwin[slot])

    neighbour(z)
    for t in range(1, nr):
        for way in range(2):
            behind, has_behind = along(way, t)[5:]
            pl.when(has_behind)(functools.partial(neighbour, behind))

    inv = 1.0 / jnp.sqrt(1.0 + jnp.sum(sq_ref[...].astype(F32), axis=1, keepdims=True))
    y = acc[...].astype(BF16)
    message = mm(y, wm_ref[...]) * inv
    sig = 1.0 / (1.0 + jnp.exp(-message))
    smooth = (message * sig).astype(BF16)
    d_message = (ds[...] * sig * (1.0 + message * (1.0 - sig)) * inv).astype(BF16)
    dz = mm_bt(d_message, wm_ref[...]).astype(BF16)
    dzb[...] = dz
    g[0] = mm_t(y, d_message).reshape(g.shape[1:]).astype(BF16)
    g[1] = mm_t(smooth, cot_ref[...]).reshape(g.shape[1:]).astype(BF16)
    smb[...] = smooth
    start(g.at[1 - c], grecv, sp, rp, {"blk": mate})

    def send_partials(shard, when=None):
        for d, side, where in ((0, 2, up), (1, 0, down)):
            qs[d, shard] = mm_t(tiles(side, shard), dzb[...]).astype(BF16)
            start_when(
                when,
                lambda d=d, where=where: (
                    qs.at[d, shard], qr.at[d, shard], sq_s.at[d, shard], sq_r.at[d, shard], {"blk": where}
                ),
            )

    for t in range(nr - 1, 0, -1):
        for way in range(2):
            far, has_far = along(way, t)[2:4]
            pl.when(has_far)(functools.partial(send_partials, far, has_far))
    send_partials(z)
    upd_ref[...] = (x_ref[...].astype(F32) + mm(smb[...], wu_ref[...])).astype(BF16)

    def pair_sum():
        copy(grecv, grecv, sp, rp, {"blk": mate}).wait_recv()
        hbuf[...] = (g[c].astype(F32) + grecv[...].astype(F32)).astype(BF16)
        for i in range(1, ny):
            start(hbuf.at[y_peer[i]], yrecv.at[i - 1], sy.at[i - 1], ry.at[i - 1], {"blk": 2 * y_peer[i] + c})

    def y_sum():
        part = hbuf[yy].astype(F32)
        for i in range(1, ny):
            place = yrecv.at[i - 1]
            copy(place, place, sy.at[i - 1], ry.at[i - 1], {"blk": mate}).wait_recv()
            part += yrecv[i - 1].astype(F32)
        h2[...] = part.astype(BF16)
        for j in range(1, nr):
            start(h2.at[others[j]], zrecv.at[j - 1], sz.at[j - 1], rz.at[j - 1], {"rows": others[j]})

    def z_sum():
        piece = h2[z].astype(F32)
        for j in range(1, nr):
            place = zrecv.at[j - 1]
            copy(place, place, sz.at[j - 1], rz.at[j - 1], {"blk": mate}).wait_recv()
            piece += zrecv[j - 1].astype(F32)
        gout[c, yy, z] = piece.astype(BF16)
        place = gout.at[c, yy, z]
        for j in range(1, nr):
            start(place, place, sa.at[j - 1], ra.at[j - 1], {"rows": others[j]})

    def z_gather():
        for j in range(1, nr):
            place = gout.at[c, yy, sources[j]]
            copy(place, place, sa.at[j - 1], ra.at[j - 1], {"blk": mate}).wait_recv()
        place = gout.at[c, yy]
        for i in range(1, ny):
            start(place, place, sb.at[i - 1], rb.at[i - 1], {"blk": 2 * y_peer[i] + c})
        start(place, place, sm.at[0], rm.at[0], {"blk": mate})

    def summed(shard):
        tot[...] = mm_t(tiles(1, shard), dzb[...])
        for d in range(2):
            place = qr.at[d, shard]
            copy(place, place, sq_s.at[d, shard], sq_r.at[d, shard], {"blk": up}).wait_recv()
            tot[...] += qr[d, shard].astype(F32)

    def add_arrived(way, t):
        place = sr.at[way, t]
        copy(place, place, st_s.at[way, t], st_r.at[way, t], {"blk": up}).wait_recv()
        tot[...] += sr[way, t].astype(F32)

    pair_sum()
    between = [y_sum, z_sum, z_gather]
    for t in range(nr - 1, 0, -1):
        for way in range(2):
            there, has_there, far, has_far, has_near, behind, has_behind = along(way, t)

            def pass_on(way=way, t=t, there=there, far=far, has_far=has_far, has_near=has_near):
                summed(far)
                if t < nr - 1:
                    pl.when(has_near)(functools.partial(add_arrived, way, t))
                ss[way, t - 1] = tot[...].astype(BF16)
                start_when(
                    has_far,
                    lambda: (
                        ss.at[way, t - 1], sr.at[way, t - 1], st_s.at[way, t - 1], st_r.at[way, t - 1],
                        {"rows": there},
                    ),
                )

            pl.when(has_far)(pass_on)
        if between:
            between.pop(0)()
    for run in between:
        run()
    summed(z)
    for way in range(2):
        has_near = along(way, 1)[4]
        pl.when(has_near)(functools.partial(add_arrived, way, 0))
    df_ref[...] = (tot[...] + cot_ref[...].astype(F32)).astype(BF16)

    for i in range(1, ny):
        place = gout.at[c, y_from[i]]
        copy(place, place, sb.at[i - 1], rb.at[i - 1], {"blk": mate}).wait_recv()
        start(place, place, sm.at[i], rm.at[i], {"blk": mate})
    for i in range(ny):
        place = gout.at[1 - c, y_from[i]]
        copy(place, place, sm.at[i], rm.at[i], {"blk": mate}).wait_recv()
    for when, make in sends:
        guarded(when, lambda make=make: copy(*make()).wait_send())


def body(features, w_message, w_update, block_index, slot_count, edge_count, cotangent):
    nr = lax.axis_size("rows")
    nb = lax.axis_size("blk")
    ny = nb // 2
    lb = block_index.shape[0]
    rows, width = features.shape
    a, sq = dense(block_index, slot_count, edge_count, nb, nr)
    pr = width // (ny * nr)
    shard = (rows, width)
    dma = pltpu.SemaphoreType.DMA
    vmem = pl.BlockSpec(memory_space=pltpu.VMEM)
    n1 = nr - 1
    updated, d_features, grads = pl.pallas_call(
        functools.partial(layer_kernel, nb, nr, lb),
        out_shape=(
            jax.ShapeDtypeStruct(shard, BF16),
            jax.ShapeDtypeStruct(shard, BF16),
            jax.ShapeDtypeStruct((2, ny, nr, pr, width), BF16),
        ),
        in_specs=[vmem] * 6,
        out_specs=(vmem,) * 3,
        scratch_shapes=[
            pltpu.VMEM((3 * nr,) + shard, BF16),
            pltpu.VMEM((2, nr) + shard, BF16),
            pltpu.VMEM((2, nr) + shard, BF16),
            pltpu.VMEM((2, n1) + shard, BF16),
            pltpu.VMEM((2, n1) + shard, BF16),
            pltpu.VMEM(shard, F32),
            pltpu.VMEM(shard, F32),
            pltpu.VMEM(shard, F32),
            pltpu.VMEM(shard, BF16),
            pltpu.VMEM(shard, BF16),
            pltpu.VMEM((2, ny, nr, pr, width), BF16),
            pltpu.VMEM((ny, nr, pr, width), BF16),
            pltpu.VMEM((ny, nr, pr, width), BF16),
            pltpu.VMEM((ny - 1, nr, pr, width), BF16),
            pltpu.VMEM((nr, pr, width), BF16),
            pltpu.VMEM((n1, pr, width), BF16),
            dma((2, n1)), dma((2, n1)),
            dma((2, nr)), dma((2, nr)),
            dma((2, nr)), dma((2, nr)),
            dma((2, n1)), dma((2, n1)),
            dma, dma,
            dma((ny - 1,)), dma((ny - 1,)),
            dma((n1,)), dma((n1,)),
            dma((n1,)), dma((n1,)),
            dma((ny - 1,)), dma((ny - 1,)),
            dma((ny,)), dma((ny,)),
        ],
        compiler_params=pltpu.CompilerParams(
            collective_id=0, has_side_effects=True, vmem_limit_bytes=48 * 1024 * 1024
        ),
    )(a, sq, features, cotangent, w_message, w_update)
    scale = 1.0 / math.sqrt(rows * nb * nr)
    grad_message = grads[0].reshape(width, width).astype(F32) * scale
    grad_update = grads[1].reshape(width, width).astype(F32) * scale
    return (updated, d_features, grad_message, grad_update)


def solution(mesh):
    placed = (
        P(("parts", "blk", "rows"), None),
        P(),
        P(),
        P(("parts", "blk", "rows"), None),
        P(("parts", "blk", "rows")),
        P(("parts", "blk", "rows"), None, None, None),
        P(("parts", "blk", "rows"), None),
    )
    return jax.shard_map(
        body,
        mesh=mesh,
        in_specs=placed,
        out_specs=(
            P(("parts", "blk", "rows"), None),
            P(("parts", "blk", "rows"), None),
            P("parts", None),
            P("parts", None),
        ),
        check_vma=False,
    )
```

```python
import functools
import math

import jax
import jax.numpy as jnp
from jax import lax
from jax.experimental import pallas as pl
from jax.experimental.pallas import tpu as pltpu
from jax.sharding import PartitionSpec as P

MESH = pl.DeviceIdType.MESH
F32 = jnp.float32
BF16 = jnp.bfloat16
SLOT_STEP = 8


def dense_kernel(nb, region_blocks, index_ref, count_ref, edge_ref, a_ref, sq_ref):
    b = pl.program_id(0)
    step = pl.program_id(1)
    r = lax.axis_index("blk")
    tile = edge_ref.shape[2]

    @pl.when((b == 0) & (step == 0))
    def _():
        a_ref[...] = jnp.zeros_like(a_ref)
        sq_ref[...] = jnp.zeros_like(sq_ref)

    rows = pl.ds(pl.multiple_of(b * tile, tile), tile)
    used = count_ref[b]
    for i in range(edge_ref.shape[1]):
        s = step * edge_ref.shape[1] + i

        @pl.when(s < used)
        def _():
            total = nb * region_blocks
            k = lax.rem(index_ref[b, s] - (r - 1) * region_blocks + 2 * total, total)
            c = edge_ref[0, i].astype(BF16)
            a_ref[k, rows, :] += c
            sq_ref[rows, :] += c * c


def dense(block_index, slot_count, edge_count, nb, nr):
    lb, slots = block_index.shape
    tile = edge_count.shape[2]
    step = SLOT_STEP if slots % SLOT_STEP == 0 else 1
    region_blocks = lb * nr
    return pl.pallas_call(
        functools.partial(dense_kernel, nb, region_blocks),
        grid=(lb, slots // step),
        out_shape=(
            jax.ShapeDtypeStruct((3 * region_blocks, lb * tile, tile), BF16),
            jax.ShapeDtypeStruct((lb * tile, tile), BF16),
        ),
        in_specs=[
            pl.BlockSpec(memory_space=pltpu.SMEM),
            pl.BlockSpec(memory_space=pltpu.SMEM),
            pl.BlockSpec((1, step, tile, tile), lambda b, s: (b, s, 0, 0)),
        ],
        out_specs=(
            pl.BlockSpec((3 * region_blocks, lb * tile, tile), lambda b, s: (0, 0, 0)),
            pl.BlockSpec((lb * tile, tile), lambda b, s: (0, 0)),
        ),
        compiler_params=pltpu.CompilerParams(vmem_limit_bytes=32 * 1024 * 1024),
    )(block_index, slot_count, edge_count)


def layer_kernel(
    nb, nr, lb,
    a_ref, sq_ref, x_ref, cot_ref, wm_ref, wu_ref,
    upd_ref, df_ref, gout,
    xwin, qs, qr, ss, sr, acc, ds, tot, dzb, smb, g, grecv, hbuf, yrecv, h2, zrecv,
    s1, r1, sf, rf, sq_s, sq_r, st_s, st_r,
    sp, rp, sy, ry, sz, rz, sa, ra, sb, rb, sm, rm,
):
    z = lax.axis_index("rows")
    r = lax.axis_index("blk")
    ny = nb // 2
    c = lax.rem(r, 2)
    yy = r // 2
    mate = yy * 2 + (1 - c)
    up, down = lax.rem(r + 1, nb), lax.rem(r + nb - 1, nb)
    others = [lax.rem(z + j, nr) for j in range(nr)]
    sources = [lax.rem(z + nr - j, nr) for j in range(nr)]
    y_peer = [lax.rem(yy + i, ny) for i in range(ny)]
    y_from = [lax.rem(yy + ny - i, ny) for i in range(ny)]

    def copy(src, dst, send, recv, where):
        return pltpu.make_async_remote_copy(
            src_ref=src, dst_ref=dst, send_sem=send, recv_sem=recv,
            device_id=where, device_id_type=MESH,
        )

    barrier = pltpu.get_barrier_semaphore()
    peers = [{"rows": others[j]} for j in range(1, nr)]
    peers += [{"blk": up}, {"blk": down}]
    peers += [{"blk": lax.rem(r + 2 * i, nb)} for i in range(1, ny)]
    for where in peers:
        pl.semaphore_signal(barrier, inc=1, device_id=where, device_id_type=MESH)
    pl.semaphore_wait(barrier, len(peers))

    sends = []

    def start(*args):
        start_when(None, lambda: args)

    def start_when(when, make):
        copy(*make()).start()
        sends.append((when, make))

    def guarded(when, run):
        if when is None:
            run()
        else:
            pl.when(when)(run)

    def forward(src, shard, h, when=None):
        for d, where in ((0, up), (1, down)):
            start_when(
                when,
                lambda d=d, where=where: (
                    src(), xwin.at[2 * d * nr + shard, h], sf.at[d, shard, h], rf.at[d, shard, h], {"blk": where}
                ),
            )

    def along(way, t):
        sign = 1 - 2 * way
        there = z + sign
        far = z + sign * t
        near = z - sign
        behind = z - sign * t
        has_there = (there >= 0) & (there < nr)
        has_far = (far >= 0) & (far < nr)
        has_near = (near >= 0) & (near < nr)
        has_behind = (behind >= 0) & (behind < nr)
        return there, has_there, far, has_far, has_near, behind, has_behind

    for h in range(lb):
        forward(lambda h=h: x_ref.at[h], z, h)
        for way in range(2):
            there, has_there = along(way, 1)[:2]

            def first(way=way, there=there, has_there=has_there, h=h):
                start_when(
                    has_there,
                    lambda: (x_ref.at[h], xwin.at[nr + z, h], s1.at[way, 0, h], r1.at[way, 0, h], {"rows": there}),
                )

            pl.when(has_there)(first)

    def flat(value):
        return value.reshape(value.shape[0] * value.shape[1], value.shape[2])

    def tiles(side, shard):
        first = (side * nr + shard) * lb
        return jnp.concatenate([a_ref[first + i] for i in range(lb)], axis=1)

    def mm(a, b):
        return jnp.dot(a, b, preferred_element_type=F32)

    def mm_t(a, b):
        return lax.dot_general(a, b, (((0,), (0,)), ((), ())), preferred_element_type=F32)

    def mm_bt(a, b):
        return lax.dot_general(a, b, (((1,), (1,)), ((), ())), preferred_element_type=F32)

    ds[...] = mm_bt(cot_ref[...], wu_ref[...])
    acc[...] = mm(tiles(1, z), flat(x_ref[...]))
    for t in range(1, nr):
        for way in range(2):
            there, has_there, far, has_far, has_near, behind, has_behind = along(way, t)

            def relay(way=way, t=t, there=there, behind=behind, when=has_there & has_behind, h=0):
                start_when(
                    when,
                    lambda: (
                        xwin.at[nr + behind, h], xwin.at[nr + behind, h],
                        s1.at[way, t, h], r1.at[way, t, h], {"rows": there},
                    ),
                )

            def use(way=way, t=t, behind=behind, has_there=has_there, has_behind=has_behind, relay=relay):
                for h in range(lb):
                    place = xwin.at[nr + behind, h]
                    copy(place, place, s1.at[way, t - 1, h], r1.at[way, t - 1, h], {"blk": up}).wait_recv()
                    if t < nr - 1:
                        pl.when(has_there)(functools.partial(relay, h=h))
                    forward(lambda h=h: xwin.at[nr + behind, h], behind, h, has_behind)
                acc[...] += mm(tiles(1, behind), flat(xwin[nr + behind]))

            pl.when(has_behind)(use)

    def neighbour(shard):
        for d, side in ((0, 0), (1, 2)):
            slot = side * nr + shard
            for h in range(lb):
                place = xwin.at[slot, h]
                copy(place, place, sf.at[d, shard, h], rf.at[d, shard, h], {"blk": up}).wait_recv()
            acc[...] += mm(tiles(side, shard), flat(xwin[slot]))

    neighbour(z)
    for t in range(1, nr):
        for way in range(2):
            behind, has_behind = along(way, t)[5:]
            pl.when(has_behind)(functools.partial(neighbour, behind))

    inv = 1.0 / jnp.sqrt(1.0 + jnp.sum(sq_ref[...].astype(F32), axis=1, keepdims=True))
    y = acc[...].astype(BF16)
    message = mm(y, wm_ref[...]) * inv
    sig = 1.0 / (1.0 + jnp.exp(-message))
    smooth = (message * sig).astype(BF16)
    d_message = (ds[...] * sig * (1.0 + message * (1.0 - sig)) * inv).astype(BF16)
    dz = mm_bt(d_message, wm_ref[...]).astype(BF16)
    dzb[...] = dz
    g[0] = mm_t(y, d_message).reshape(g.shape[1:]).astype(BF16)
    g[1] = mm_t(smooth, cot_ref[...]).reshape(g.shape[1:]).astype(BF16)
    smb[...] = smooth
    start(g.at[1 - c], grecv, sp, rp, {"blk": mate})

    def send_partials(shard, when=None):
        for d, side, where in ((0, 2, up), (1, 0, down)):
            qs[d, shard] = mm_t(tiles(side, shard), dzb[...]).reshape(x_ref.shape).astype(BF16)
            for h in range(lb):
                start_when(
                    when,
                    lambda d=d, where=where, h=h: (
                        qs.at[d, shard, h], qr.at[d, shard, h],
                        sq_s.at[d, shard, h], sq_r.at[d, shard, h], {"blk": where},
                    ),
                )

    def send_step(t):
        if t == 0:
            send_partials(z)
            return
        for way in range(2):
            far, has_far = along(way, t)[2:4]
            pl.when(has_far)(functools.partial(send_partials, far, has_far))

    def pair_sum():
        copy(grecv, grecv, sp, rp, {"blk": mate}).wait_recv()
        hbuf[...] = (g[c].astype(F32) + grecv[...].astype(F32)).astype(BF16)
        for i in range(1, ny):
            start(hbuf.at[y_peer[i]], yrecv.at[i - 1], sy.at[i - 1], ry.at[i - 1], {"blk": 2 * y_peer[i] + c})

    def y_sum():
        part = hbuf[yy].astype(F32)
        for i in range(1, ny):
            place = yrecv.at[i - 1]
            copy(place, place, sy.at[i - 1], ry.at[i - 1], {"blk": mate}).wait_recv()
            part += yrecv[i - 1].astype(F32)
        h2[...] = part.astype(BF16)
        for j in range(1, nr):
            start(h2.at[others[j]], zrecv.at[j - 1], sz.at[j - 1], rz.at[j - 1], {"rows": others[j]})

    def z_sum():
        piece = h2[z].astype(F32)
        for j in range(1, nr):
            place = zrecv.at[j - 1]
            copy(place, place, sz.at[j - 1], rz.at[j - 1], {"blk": mate}).wait_recv()
            piece += zrecv[j - 1].astype(F32)
        gout[c, yy, z] = piece.astype(BF16)
        place = gout.at[c, yy, z]
        for j in range(1, nr):
            start(place, place, sa.at[j - 1], ra.at[j - 1], {"rows": others[j]})

    def z_gather():
        for j in range(1, nr):
            place = gout.at[c, yy, sources[j]]
            copy(place, place, sa.at[j - 1], ra.at[j - 1], {"blk": mate}).wait_recv()
        place = gout.at[c, yy]
        for i in range(1, ny):
            start(place, place, sb.at[i - 1], rb.at[i - 1], {"blk": 2 * y_peer[i] + c})
        start(place, place, sm.at[0], rm.at[0], {"blk": mate})

    def own_part(shard):
        tot[...] = mm_t(tiles(1, shard), dzb[...]).reshape(tot.shape)

    def add_partials(shard, h):
        for d in range(2):
            place = qr.at[d, shard, h]
            copy(place, place, sq_s.at[d, shard, h], sq_r.at[d, shard, h], {"blk": up}).wait_recv()
            tot[h] += qr[d, shard, h].astype(F32)

    def add_arrived(way, t, h):
        place = sr.at[way, t, h]
        copy(place, place, st_s.at[way, t, h], st_r.at[way, t, h], {"blk": up}).wait_recv()
        tot[h] += sr[way, t, h].astype(F32)

    send_step(nr - 1)
    pair_sum()
    send_step(nr - 2)
    upd_ref[...] = (flat(x_ref[...]).astype(F32) + mm(smb[...], wu_ref[...])).astype(BF16)
    between = [y_sum, z_sum, z_gather]
    for t in range(nr - 1, 0, -1):
        if t >= 2:
            send_step(t - 2)
        for way in range(2):
            there, has_there, far, has_far, has_near, behind, has_behind = along(way, t)

            def pass_on(way=way, t=t, there=there, far=far, has_far=has_far, has_near=has_near):
                own_part(far)
                for h in range(lb):
                    add_partials(far, h)
                    if t < nr - 1:
                        pl.when(has_near)(functools.partial(add_arrived, way, t, h))
                    ss[way, t - 1, h] = tot[h].astype(BF16)
                    start_when(
                        has_far,
                        lambda h=h: (
                            ss.at[way, t - 1, h], sr.at[way, t - 1, h],
                            st_s.at[way, t - 1, h], st_r.at[way, t - 1, h], {"rows": there},
                        ),
                    )

            pl.when(has_far)(pass_on)
        if between:
            between.pop(0)()
    for run in between:
        run()
    own_part(z)
    for h in range(lb):
        add_partials(z, h)
        for way in range(2):
            has_near = along(way, 1)[4]
            pl.when(has_near)(functools.partial(add_arrived, way, 0, h))
    df_ref[...] = (flat(tot[...]) + cot_ref[...].astype(F32)).astype(BF16)

    for i in range(1, ny):
        place = gout.at[c, y_from[i]]
        copy(place, place, sb.at[i - 1], rb.at[i - 1], {"blk": mate}).wait_recv()
        start(place, place, sm.at[i], rm.at[i], {"blk": mate})
    for i in range(ny):
        place = gout.at[1 - c, y_from[i]]
        copy(place, place, sm.at[i], rm.at[i], {"blk": mate}).wait_recv()
    for when, make in sends:
        guarded(when, lambda make=make: copy(*make()).wait_send())


def body(features, w_message, w_update, block_index, slot_count, edge_count, cotangent):
    nr = lax.axis_size("rows")
    nb = lax.axis_size("blk")
    ny = nb // 2
    lb = block_index.shape[0]
    rows, width = features.shape
    a, sq = dense(block_index, slot_count, edge_count, nb, nr)
    pr = width // (ny * nr)
    shard = (rows, width)
    halves = (lb, rows // lb, width)
    dma = pltpu.SemaphoreType.DMA
    vmem = pl.BlockSpec(memory_space=pltpu.VMEM)
    n1 = nr - 1
    updated, d_features, grads = pl.pallas_call(
        functools.partial(layer_kernel, nb, nr, lb),
        out_shape=(
            jax.ShapeDtypeStruct(shard, BF16),
            jax.ShapeDtypeStruct(shard, BF16),
            jax.ShapeDtypeStruct((2, ny, nr, pr, width), BF16),
        ),
        in_specs=[vmem] * 6,
        out_specs=(vmem,) * 3,
        scratch_shapes=[
            pltpu.VMEM((3 * nr,) + halves, BF16),
            pltpu.VMEM((2, nr) + halves, BF16),
            pltpu.VMEM((2, nr) + halves, BF16),
            pltpu.VMEM((2, n1) + halves, BF16),
            pltpu.VMEM((2, n1) + halves, BF16),
            pltpu.VMEM(shard, F32),
            pltpu.VMEM(shard, F32),
            pltpu.VMEM(halves, F32),
            pltpu.VMEM(shard, BF16),
            pltpu.VMEM(shard, BF16),
            pltpu.VMEM((2, ny, nr, pr, width), BF16),
            pltpu.VMEM((ny, nr, pr, width), BF16),
            pltpu.VMEM((ny, nr, pr, width), BF16),
            pltpu.VMEM((ny - 1, nr, pr, width), BF16),
            pltpu.VMEM((nr, pr, width), BF16),
            pltpu.VMEM((n1, pr, width), BF16),
            dma((2, n1, lb)), dma((2, n1, lb)),
            dma((2, nr, lb)), dma((2, nr, lb)),
            dma((2, nr, lb)), dma((2, nr, lb)),
            dma((2, n1, lb)), dma((2, n1, lb)),
            dma, dma,
            dma((ny - 1,)), dma((ny - 1,)),
            dma((n1,)), dma((n1,)),
            dma((n1,)), dma((n1,)),
            dma((ny - 1,)), dma((ny - 1,)),
            dma((ny,)), dma((ny,)),
        ],
        compiler_params=pltpu.CompilerParams(
            collective_id=0, has_side_effects=True, vmem_limit_bytes=48 * 1024 * 1024
        ),
    )(a, sq, features.reshape(halves), cotangent, w_message, w_update)
    scale = 1.0 / math.sqrt(rows * nb * nr)
    grad_message = grads[0].reshape(width, width).astype(F32) * scale
    grad_update = grads[1].reshape(width, width).astype(F32) * scale
    return (updated, d_features, grad_message, grad_update)


def solution(mesh):
    placed = (
        P(("parts", "blk", "rows"), None),
        P(),
        P(),
        P(("parts", "blk", "rows"), None),
        P(("parts", "blk", "rows")),
        P(("parts", "blk", "rows"), None, None, None),
        P(("parts", "blk", "rows"), None),
    )
    return jax.shard_map(
        body,
        mesh=mesh,
        in_specs=placed,
        out_specs=(
            P(("parts", "blk", "rows"), None),
            P(("parts", "blk", "rows"), None),
            P("parts", None),
            P("parts", None),
        ),
        check_vma=False,
    )
```

```python
import functools
import math

import jax
import jax.numpy as jnp
from jax import lax
from jax.experimental import pallas as pl
from jax.experimental.pallas import tpu as pltpu
from jax.sharding import PartitionSpec as P

MESH = pl.DeviceIdType.MESH
F32 = jnp.float32
BF16 = jnp.bfloat16
SLOT_STEP = 40


def dense_kernel(nb, region_blocks, index_ref, count_ref, edge_ref, a_ref, sq_ref):
    b = pl.program_id(0)
    step = pl.program_id(1)
    r = lax.axis_index("blk")
    tile = edge_ref.shape[2]

    @pl.when((b == 0) & (step == 0))
    def _():
        a_ref[...] = jnp.zeros_like(a_ref)
        sq_ref[...] = jnp.zeros_like(sq_ref)

    rows = pl.ds(pl.multiple_of(b * tile, tile), tile)
    used = count_ref[b]
    for i in range(edge_ref.shape[1]):
        s = step * edge_ref.shape[1] + i

        @pl.when(s < used)
        def _():
            total = nb * region_blocks
            k = lax.rem(index_ref[b, s] - (r - 1) * region_blocks + 2 * total, total)
            c = edge_ref[0, i].astype(BF16)
            a_ref[k, rows, :] += c
            sq_ref[rows, :] += c * c


def dense(block_index, slot_count, edge_count, nb, nr):
    lb, slots = block_index.shape
    tile = edge_count.shape[2]
    step = SLOT_STEP if slots % SLOT_STEP == 0 else 1
    region_blocks = lb * nr
    return pl.pallas_call(
        functools.partial(dense_kernel, nb, region_blocks),
        grid=(lb, slots // step),
        out_shape=(
            jax.ShapeDtypeStruct((3 * region_blocks, lb * tile, tile), BF16),
            jax.ShapeDtypeStruct((lb * tile, tile), BF16),
        ),
        in_specs=[
            pl.BlockSpec(memory_space=pltpu.SMEM),
            pl.BlockSpec(memory_space=pltpu.SMEM),
            pl.BlockSpec((1, step, tile, tile), lambda b, s: (b, s, 0, 0)),
        ],
        out_specs=(
            pl.BlockSpec((3 * region_blocks, lb * tile, tile), lambda b, s: (0, 0, 0)),
            pl.BlockSpec((lb * tile, tile), lambda b, s: (0, 0)),
        ),
        compiler_params=pltpu.CompilerParams(vmem_limit_bytes=32 * 1024 * 1024),
    )(block_index, slot_count, edge_count)


def layer_kernel(
    nb, nr, lb,
    a_ref, sq_ref, x_ref, cot_ref, wm_ref, wu_ref,
    upd_ref, df_ref, gout,
    xwin, qs, qr, ss, sr, acc, ds, tot, dzb, smb, g, grecv, hbuf, yrecv, h2, zrecv,
    s1, r1, sf, rf, sq_s, sq_r, st_s, st_r,
    sp, rp, sy, ry, sz, rz, sa, ra, sb, rb, sm, rm,
):
    z = lax.axis_index("rows")
    r = lax.axis_index("blk")
    ny = nb // 2
    c = lax.rem(r, 2)
    yy = r // 2
    mate = yy * 2 + (1 - c)
    up, down = lax.rem(r + 1, nb), lax.rem(r + nb - 1, nb)
    others = [lax.rem(z + j, nr) for j in range(nr)]
    sources = [lax.rem(z + nr - j, nr) for j in range(nr)]
    y_peer = [lax.rem(yy + i, ny) for i in range(ny)]
    y_from = [lax.rem(yy + ny - i, ny) for i in range(ny)]

    def copy(src, dst, send, recv, where):
        return pltpu.make_async_remote_copy(
            src_ref=src, dst_ref=dst, send_sem=send, recv_sem=recv,
            device_id=where, device_id_type=MESH,
        )

    barrier = pltpu.get_barrier_semaphore()
    peers = [{"rows": others[j]} for j in range(1, nr)]
    peers += [{"blk": up}, {"blk": down}]
    peers += [{"blk": lax.rem(r + 2 * i, nb)} for i in range(1, ny)]
    for where in peers:
        pl.semaphore_signal(barrier, inc=1, device_id=where, device_id_type=MESH)
    pl.semaphore_wait(barrier, len(peers))

    sends = []

    def start(*args):
        start_when(None, lambda: args)

    def start_when(when, make):
        copy(*make()).start()
        sends.append((when, make))

    def guarded(when, run):
        if when is None:
            run()
        else:
            pl.when(when)(run)

    def forward(src, shard, h, when=None):
        for d, where in ((0, up), (1, down)):
            start_when(
                when,
                lambda d=d, where=where: (
                    src(), xwin.at[2 * d * nr + shard, h], sf.at[d, shard, h], rf.at[d, shard, h], {"blk": where}
                ),
            )

    def along(way, t):
        sign = 1 - 2 * way
        there = z + sign
        far = z + sign * t
        near = z - sign
        behind = z - sign * t
        has_there = (there >= 0) & (there < nr)
        has_far = (far >= 0) & (far < nr)
        has_near = (near >= 0) & (near < nr)
        has_behind = (behind >= 0) & (behind < nr)
        return there, has_there, far, has_far, has_near, behind, has_behind

    for h in range(lb):
        forward(lambda h=h: x_ref.at[h], z, h)
        for way in range(2):
            there, has_there = along(way, 1)[:2]

            def first(way=way, there=there, has_there=has_there, h=h):
                start_when(
                    has_there,
                    lambda: (x_ref.at[h], xwin.at[nr + z, h], s1.at[way, 0, h], r1.at[way, 0, h], {"rows": there}),
                )

            pl.when(has_there)(first)

    def flat(value):
        return value.reshape(value.shape[0] * value.shape[1], value.shape[2])

    def tiles(side, shard):
        first = (side * nr + shard) * lb
        return jnp.concatenate([a_ref[first + i] for i in range(lb)], axis=1)

    def mm(a, b):
        return jnp.dot(a, b, preferred_element_type=F32)

    def mm_t(a, b):
        return lax.dot_general(a, b, (((0,), (0,)), ((), ())), preferred_element_type=F32)

    def mm_bt(a, b):
        return lax.dot_general(a, b, (((1,), (1,)), ((), ())), preferred_element_type=F32)

    ds[...] = mm_bt(cot_ref[...], wu_ref[...])
    acc[...] = mm(tiles(1, z), flat(x_ref[...]))
    for t in range(1, nr):
        for way in range(2):
            there, has_there, far, has_far, has_near, behind, has_behind = along(way, t)

            def relay(way=way, t=t, there=there, behind=behind, when=has_there & has_behind, h=0):
                start_when(
                    when,
                    lambda: (
                        xwin.at[nr + behind, h], xwin.at[nr + behind, h],
                        s1.at[way, t, h], r1.at[way, t, h], {"rows": there},
                    ),
                )

            def use(way=way, t=t, behind=behind, has_there=has_there, has_behind=has_behind, relay=relay):
                for h in range(lb):
                    place = xwin.at[nr + behind, h]
                    copy(place, place, s1.at[way, t - 1, h], r1.at[way, t - 1, h], {"blk": up}).wait_recv()
                    if t < nr - 1:
                        pl.when(has_there)(functools.partial(relay, h=h))
                    forward(lambda h=h: xwin.at[nr + behind, h], behind, h, has_behind)
                acc[...] += mm(tiles(1, behind), flat(xwin[nr + behind]))

            pl.when(has_behind)(use)

    def neighbour(shard):
        for d, side in ((0, 0), (1, 2)):
            slot = side * nr + shard
            for h in range(lb):
                place = xwin.at[slot, h]
                copy(place, place, sf.at[d, shard, h], rf.at[d, shard, h], {"blk": up}).wait_recv()
            acc[...] += mm(tiles(side, shard), flat(xwin[slot]))

    neighbour(z)
    for t in range(1, nr):
        for way in range(2):
            behind, has_behind = along(way, t)[5:]
            pl.when(has_behind)(functools.partial(neighbour, behind))

    inv = 1.0 / jnp.sqrt(1.0 + jnp.sum(sq_ref[...].astype(F32), axis=1, keepdims=True))
    y = acc[...].astype(BF16)
    message = mm(y, wm_ref[...]) * inv
    sig = 1.0 / (1.0 + jnp.exp(-message))
    smooth = (message * sig).astype(BF16)
    d_message = (ds[...] * sig * (1.0 + message * (1.0 - sig)) * inv).astype(BF16)
    dz = mm_bt(d_message, wm_ref[...]).astype(BF16)
    dzb[...] = dz
    g[0] = mm_t(y, d_message).reshape(g.shape[1:]).astype(BF16)
    g[1] = mm_t(smooth, cot_ref[...]).reshape(g.shape[1:]).astype(BF16)
    smb[...] = smooth
    start(g.at[1 - c], grecv, sp, rp, {"blk": mate})

    def send_partials(shard, when=None):
        for d, side, where in ((0, 2, up), (1, 0, down)):
            qs[d, shard] = mm_t(tiles(side, shard), dzb[...]).reshape(x_ref.shape).astype(BF16)
            for h in range(lb):
                start_when(
                    when,
                    lambda d=d, where=where, h=h: (
                        qs.at[d, shard, h], qr.at[d, shard, h],
                        sq_s.at[d, shard, h], sq_r.at[d, shard, h], {"blk": where},
                    ),
                )

    def send_step(t):
        if t == 0:
            send_partials(z)
            return
        for way in range(2):
            far, has_far = along(way, t)[2:4]
            pl.when(has_far)(functools.partial(send_partials, far, has_far))

    def pair_sum():
        copy(grecv, grecv, sp, rp, {"blk": mate}).wait_recv()
        hbuf[...] = (g[c].astype(F32) + grecv[...].astype(F32)).astype(BF16)
        for i in range(1, ny):
            start(hbuf.at[y_peer[i]], yrecv.at[i - 1], sy.at[i - 1], ry.at[i - 1], {"blk": 2 * y_peer[i] + c})

    def y_sum():
        part = hbuf[yy].astype(F32)
        for i in range(1, ny):
            place = yrecv.at[i - 1]
            copy(place, place, sy.at[i - 1], ry.at[i - 1], {"blk": mate}).wait_recv()
            part += yrecv[i - 1].astype(F32)
        h2[...] = part.astype(BF16)
        for j in range(1, nr):
            start(h2.at[others[j]], zrecv.at[j - 1], sz.at[j - 1], rz.at[j - 1], {"rows": others[j]})

    def z_sum():
        piece = h2[z].astype(F32)
        for j in range(1, nr):
            place = zrecv.at[j - 1]
            copy(place, place, sz.at[j - 1], rz.at[j - 1], {"blk": mate}).wait_recv()
            piece += zrecv[j - 1].astype(F32)
        gout[c, yy, z] = piece.astype(BF16)
        place = gout.at[c, yy, z]
        for j in range(1, nr):
            start(place, place, sa.at[j - 1], ra.at[j - 1], {"rows": others[j]})

    def z_gather():
        for j in range(1, nr):
            place = gout.at[c, yy, sources[j]]
            copy(place, place, sa.at[j - 1], ra.at[j - 1], {"blk": mate}).wait_recv()
        place = gout.at[c, yy]
        for i in range(1, ny):
            start(place, place, sb.at[i - 1], rb.at[i - 1], {"blk": 2 * y_peer[i] + c})
        start(place, place, sm.at[0], rm.at[0], {"blk": mate})

    def own_part(shard):
        tot[...] = mm_t(tiles(1, shard), dzb[...]).reshape(tot.shape)

    def add_partials(shard, h):
        for d in range(2):
            place = qr.at[d, shard, h]
            copy(place, place, sq_s.at[d, shard, h], sq_r.at[d, shard, h], {"blk": up}).wait_recv()
            tot[h] += qr[d, shard, h].astype(F32)

    def add_arrived(way, t, h):
        place = sr.at[way, t, h]
        copy(place, place, st_s.at[way, t, h], st_r.at[way, t, h], {"blk": up}).wait_recv()
        tot[h] += sr[way, t, h].astype(F32)

    send_step(nr - 1)
    pair_sum()
    send_step(nr - 2)
    upd_ref[...] = (flat(x_ref[...]).astype(F32) + mm(smb[...], wu_ref[...])).astype(BF16)
    between = [y_sum, z_sum, z_gather]
    for t in range(nr - 1, 0, -1):
        if t >= 2:
            send_step(t - 2)
        for way in range(2):
            there, has_there, far, has_far, has_near, behind, has_behind = along(way, t)

            def pass_on(way=way, t=t, there=there, far=far, has_far=has_far, has_near=has_near):
                own_part(far)
                for h in range(lb):
                    add_partials(far, h)
                    if t < nr - 1:
                        pl.when(has_near)(functools.partial(add_arrived, way, t, h))
                    ss[way, t - 1, h] = tot[h].astype(BF16)
                    start_when(
                        has_far,
                        lambda h=h: (
                            ss.at[way, t - 1, h], sr.at[way, t - 1, h],
                            st_s.at[way, t - 1, h], st_r.at[way, t - 1, h], {"rows": there},
                        ),
                    )

            pl.when(has_far)(pass_on)
        if between:
            between.pop(0)()
    for run in between:
        run()
    own_part(z)
    for h in range(lb):
        add_partials(z, h)
        for way in range(2):
            has_near = along(way, 1)[4]
            pl.when(has_near)(functools.partial(add_arrived, way, 0, h))
    df_ref[...] = (flat(tot[...]) + cot_ref[...].astype(F32)).astype(BF16)

    for i in range(1, ny):
        place = gout.at[c, y_from[i]]
        copy(place, place, sb.at[i - 1], rb.at[i - 1], {"blk": mate}).wait_recv()
        start(place, place, sm.at[i], rm.at[i], {"blk": mate})
    for i in range(ny):
        place = gout.at[1 - c, y_from[i]]
        copy(place, place, sm.at[i], rm.at[i], {"blk": mate}).wait_recv()
    for when, make in sends:
        guarded(when, lambda make=make: copy(*make()).wait_send())


def body(features, w_message, w_update, block_index, slot_count, edge_count, cotangent):
    nr = lax.axis_size("rows")
    nb = lax.axis_size("blk")
    ny = nb // 2
    lb = block_index.shape[0]
    rows, width = features.shape
    a, sq = dense(block_index, slot_count, edge_count, nb, nr)
    pr = width // (ny * nr)
    shard = (rows, width)
    halves = (lb, rows // lb, width)
    dma = pltpu.SemaphoreType.DMA
    vmem = pl.BlockSpec(memory_space=pltpu.VMEM)
    n1 = nr - 1
    updated, d_features, grads = pl.pallas_call(
        functools.partial(layer_kernel, nb, nr, lb),
        out_shape=(
            jax.ShapeDtypeStruct(shard, BF16),
            jax.ShapeDtypeStruct(shard, BF16),
            jax.ShapeDtypeStruct((2, ny, nr, pr, width), BF16),
        ),
        in_specs=[vmem] * 6,
        out_specs=(vmem,) * 3,
        scratch_shapes=[
            pltpu.VMEM((3 * nr,) + halves, BF16),
            pltpu.VMEM((2, nr) + halves, BF16),
            pltpu.VMEM((2, nr) + halves, BF16),
            pltpu.VMEM((2, n1) + halves, BF16),
            pltpu.VMEM((2, n1) + halves, BF16),
            pltpu.VMEM(shard, F32),
            pltpu.VMEM(shard, F32),
            pltpu.VMEM(halves, F32),
            pltpu.VMEM(shard, BF16),
            pltpu.VMEM(shard, BF16),
            pltpu.VMEM((2, ny, nr, pr, width), BF16),
            pltpu.VMEM((ny, nr, pr, width), BF16),
            pltpu.VMEM((ny, nr, pr, width), BF16),
            pltpu.VMEM((ny - 1, nr, pr, width), BF16),
            pltpu.VMEM((nr, pr, width), BF16),
            pltpu.VMEM((n1, pr, width), BF16),
            dma((2, n1, lb)), dma((2, n1, lb)),
            dma((2, nr, lb)), dma((2, nr, lb)),
            dma((2, nr, lb)), dma((2, nr, lb)),
            dma((2, n1, lb)), dma((2, n1, lb)),
            dma, dma,
            dma((ny - 1,)), dma((ny - 1,)),
            dma((n1,)), dma((n1,)),
            dma((n1,)), dma((n1,)),
            dma((ny - 1,)), dma((ny - 1,)),
            dma((ny,)), dma((ny,)),
        ],
        compiler_params=pltpu.CompilerParams(
            collective_id=0, has_side_effects=True, vmem_limit_bytes=48 * 1024 * 1024
        ),
    )(a, sq, features.reshape(halves), cotangent, w_message, w_update)
    scale = 1.0 / math.sqrt(rows * nb * nr)
    grad_message = grads[0].reshape(width, width).astype(F32) * scale
    grad_update = grads[1].reshape(width, width).astype(F32) * scale
    return (updated, d_features, grad_message, grad_update)


def solution(mesh):
    placed = (
        P(("parts", "blk", "rows"), None),
        P(),
        P(),
        P(("parts", "blk", "rows"), None),
        P(("parts", "blk", "rows")),
        P(("parts", "blk", "rows"), None, None, None),
        P(("parts", "blk", "rows"), None),
    )
    return jax.shard_map(
        body,
        mesh=mesh,
        in_specs=placed,
        out_specs=(
            P(("parts", "blk", "rows"), None),
            P(("parts", "blk", "rows"), None),
            P("parts", None),
            P("parts", None),
        ),
        check_vma=False,
    )
```
